32 devices in a mesh: groups: 2 (over x), row: 2 (over core), col: 8 (over z, y).
Axes of the slice: x: 2, y: 2, z: 4, core: 2. Of those that a mesh axis runs over, the one named last changes fastest.
Arguments:
- payload: bfloat16 [2, 768, 3584], P(None, ('groups', 'row', 'col')), parts along dimension 1, may hold values from -448 to 448
- block_scales: bfloat16 [2, 768, 28], P(None, ('groups', 'row', 'col')), parts along dimension 1, may hold values from 0.0049743652 to 0.049804688
- expert_ids: int32 [2, 768, 8], P(None, ('groups', 'row', 'col')), parts along dimension 1, may hold values from 0 to 15, all different within a row; in each aligned block of 24 rows (0 to 23, 24 to 47, ..., all dimensions but the last counted through in order) at most 12 rows name the same one
- gate_codes: int32 [2, 768, 8], P(None, ('groups', 'row', 'col')), parts along dimension 1, may hold values from 1 to 255
- w_gate: bfloat16 [16, 3584, 1024], P(('row', 'col')), may hold values from -0.09375 to 0.09375
- w_up: bfloat16 [16, 3584, 1024], P(('row', 'col')), may hold values from -0.09375 to 0.09375
- w_down: bfloat16 [16, 1024, 3584], P(('row', 'col')), may hold values from -0.1875 to 0.1875
Outputs:
- mixed: bfloat16 [2, 768, 3584], P(None, ('groups', 'row', 'col')), parts along dimension 1
The draws below stay inside these ranges and needn't reach their ends.
There are 2 independent parts, one for each index of `groups`. The reference program is written for one: setup_inputs(seed, part) draws one part's arguments, and reference() takes and returns one part's arrays. A program takes and returns all parts, laid end to end along the dimension named above; an argument that names none is the same for every part. Nothing has to cross between parts.
Inputs may be any that keep to these rules, and one draw needn't show every extreme that they name: `expert_ids`: each token names 8 different experts; in each micro-batch the 24 tokens of one device name no expert more than 12 times, a bound that some block reaches.
All inputs are finite; a program needn't handle non-finite values.
Results may differ from the reference program's by a relative error of at most 0.008.
Values may be sent and summed in bfloat16 or wider, within the bound.
A program may use at most 128 MiB of HBM per device.

```python
import math
import jax
import jax.numpy as jnp
import numpy as np
from jax import lax

D = 3584
FW = 1024
TOP = 8
MICRO = 2
MB_TOK = 24
CAP = 12
NBLK = 28
EXPERTS = 16
TOKENS = 384
N_ROW = 2
N_COL = 8


def with_ends(entries, stream_key, low, high):
    shape = entries.shape
    index_at = [jax.random.randint(jax.random.fold_in(stream_key, axis), (), 0, shape[axis]) for axis in range(len(shape))]
    entries = entries.at[tuple(index_at)].set(low)
    longest = shape.index(max(shape))
    index_at[longest] = (index_at[longest] + 1) % shape[longest]
    return entries.at[tuple(index_at)].set(high)


def block_levels(rng, shape, cuts, low, largest):
    level = 1.0
    for dim, shards_of in cuts:
        heights = jax.random.uniform(jax.random.fold_in(jax.random.fold_in(rng, 6), dim), (shards_of,), jnp.float32, low / len(cuts), largest / len(cuts))
        level = level * jnp.repeat(jnp.exp(heights), shape[dim] // shards_of).reshape((-1,) + (1,) * (len(shape) - 1 - dim))
    return level


def routed_block(key, own, number, rows, count, top, reach, skew):
    ranking = jax.random.permutation(key, count)
    crowded, usual = portions_of(count, rows * top, reach, skew, True), portions_of(count, rows * top, reach, skew, False)
    places = jnp.arange(count)

    def named(sizes, offset_by):
        used = int((sizes > 0).sum())
        fixed = max(1, used // 4)
        passed = fixed + (places - fixed + offset_by * (used - fixed)) % max(1, count - fixed)
        return jnp.zeros((count,), jnp.int32).at[ranking[jnp.where(places < fixed, places, passed)]].set(jnp.asarray(sizes, jnp.int32))

    sizes = jnp.where(number % 4 == 0, named(crowded, number // 4), named(usual, number - number // 4 - 1))
    mixed = jax.random.permutation(jax.random.fold_in(own, 3), count)
    source_of, sink = mixed[0:count // 2 * 2:2], mixed[1:count // 2 * 2:2]
    margin = jnp.minimum(sizes[source_of] - 1, reach - sizes[sink]) // 2
    margin = jnp.where((source_of == ranking[0]) | (sink == ranking[0]) | (sizes[sink] == 0), 0, jnp.maximum(margin, 0))
    passed = jax.random.randint(jax.random.fold_in(own, 4), (count // 2,), 0, 1 << 20) % (margin + 1)
    sizes = sizes.at[source_of].add(-passed).at[sink].add(passed)
    labels = jnp.searchsorted(jnp.cumsum(sizes), jnp.arange(rows * top), side="right").astype(jnp.int32)
    grid = labels.reshape(top, rows).T
    grid = grid[jax.random.permutation(jax.random.fold_in(own, 1), rows)]
    offset_by = jax.random.randint(jax.random.fold_in(own, 2), (rows, 1), 0, top)
    return jnp.take_along_axis(grid, (jnp.arange(top)[None, :] + offset_by) % top, axis=1)


def portions_of(count, total, reach, skew, full):
    portions = [(1 << 20) // math.isqrt(grade ** skew) + 1 for grade in range(1, count + 1)]
    largest = reach if full else min(reach, max(-(-total // count), total * portions[0] // sum(portions)))
    least = 1 if total - largest >= count - 1 else 0
    given, spare = [largest] + [least] * (count - 1), total - largest - least * (count - 1)
    while spare > 0:
        movable = [i for i in range(1, count) if given[i] < largest] or [i for i in range(1, count) if given[i] < reach]
        mass, budget = sum([portions[i] for i in movable]), spare
        for i in movable:
            addition = min(reach - given[i], max(1, budget * portions[i] // mass), spare)
            given[i] = given[i] + addition
            spare = spare - addition
    return np.array(given)


def bell_draw(key, dims, scale, limit, shards=(), held_as=jnp.bfloat16):
    result = jax.random.normal(key, dims, jnp.float32) * scale
    if len(shards) > 0:
        result = block_levels(key, dims, shards, -0.22, 0.18) * result
    return jnp.clip(result, min=-limit, max=limit).astype(held_as)


def setup_inputs(seed: int = 0, part: int = 0) -> dict:
    keys = jax.random.split(jax.random.key(seed), 8)
    own_keys = jax.random.split(jax.random.fold_in(keys[7], part), 8)
    payload = bell_draw(own_keys[0], (MICRO, TOKENS, D), 64.0, 448.0, ((1, 16),))
    block_scales = jnp.clip(jnp.exp(math.log(0.049804688) - 2.3038113 * jax.random.uniform(own_keys[1], (MICRO, TOKENS, NBLK), jnp.float32) ** block_levels(own_keys[1], (MICRO, TOKENS, NBLK), ((1, 16),), -0.2, 0.2)), 0.0049743652, 0.049804688).astype(jnp.bfloat16)
    expert_ids_keys = jax.random.split(jax.random.fold_in(own_keys[2], 1), MICRO * TOKENS // MB_TOK)
    expert_ids_turns = jax.random.permutation(jax.random.fold_in(own_keys[2], 3), MICRO * TOKENS // MB_TOK)
    expert_ids = jax.vmap(lambda own, number: routed_block(jax.random.fold_in(own_keys[2], 2), own, number, MB_TOK, EXPERTS, TOP, CAP, 2))(expert_ids_keys, expert_ids_turns).reshape((MICRO, TOKENS, TOP))
    gate_codes = with_ends(jax.random.randint(own_keys[3], (MICRO, TOKENS, TOP), 1, 256), jax.random.fold_in(own_keys[3], 1), 1, 255).astype(jnp.int32)
    w_gate = bell_draw(keys[4], (EXPERTS, D, FW), D ** -0.5, 0.09375, ((0, 16),))
    w_up = bell_draw(keys[5], (EXPERTS, D, FW), D ** -0.5, 0.09375, ((0, 16),))
    w_down = bell_draw(keys[6], (EXPERTS, FW, D), FW ** -0.5, 0.1875, ((0, 16),))
    return dict(payload=payload, block_scales=block_scales, expert_ids=expert_ids, gate_codes=gate_codes, w_gate=w_gate, w_up=w_up, w_down=w_down)


def dequantize(values, block_scales):
    shaped = values.astype(jnp.float32).reshape(values.shape[:-1] + (block_scales.shape[-1], 128))
    scaled = shaped * block_scales.astype(jnp.float32)[..., None]
    return scaled.reshape(values.shape).astype(jnp.bfloat16)


def expert_rows(inputs, gate_matrix, up_matrix, down_matrix):
    gate = jnp.dot(inputs, gate_matrix, preferred_element_type=jnp.float32)
    upward = jnp.dot(inputs, up_matrix, preferred_element_type=jnp.float32)
    hidden = (jax.nn.silu(gate) * upward).astype(jnp.bfloat16)
    return jnp.dot(hidden, down_matrix, preferred_element_type=jnp.float32).astype(jnp.bfloat16)


def block_slots(choices, expert_count):
    catalog = jnp.arange(expert_count, dtype=jnp.int32)
    named = (choices[..., None] == catalog).astype(jnp.int32)
    per_token = jnp.sum(named, axis=-2).astype(jnp.int32)
    before = (jnp.cumsum(per_token, axis=-2) - per_token).astype(jnp.int32)
    return jnp.sum(named * before[..., None, :], axis=-1).astype(jnp.int32)


def apply_expert(operands):
    return expert_rows(operands[0], operands[1], operands[2], operands[3])


def reference(payload, block_scales, expert_ids, gate_codes, w_gate, w_up, w_down):
    device_count = N_ROW * N_COL
    dequant = dequantize(payload, block_scales)
    blocks = expert_ids.reshape(MICRO, device_count, MB_TOK, TOP)
    slots = block_slots(blocks, EXPERTS)
    micro_ids = jnp.arange(MICRO, dtype=jnp.int32)[:, None, None, None]
    sources = jnp.arange(device_count, dtype=jnp.int32)[None, :, None, None]
    position = (((blocks * MICRO + micro_ids) * device_count + sources) * CAP + slots).astype(jnp.int32)
    position = position.reshape(-1)
    spread = jnp.broadcast_to(dequant.reshape(MICRO, device_count, MB_TOK, 1, D),
                              (MICRO, device_count, MB_TOK, TOP, D)).reshape(-1, D)
    buffer = jnp.zeros((EXPERTS * MICRO * device_count * CAP, D), jnp.bfloat16).at[position].set(spread)
    buffer = buffer.reshape(EXPERTS, MICRO * device_count * CAP, D)
    outputs = lax.map(apply_expert, (buffer, w_gate, w_up, w_down))
    picked = outputs.reshape(-1, D)[position].reshape(MICRO, device_count, MB_TOK, TOP, D)
    codes = gate_codes.astype(jnp.float32)
    weights = (codes / jnp.sum(codes, axis=-1, keepdims=True)).reshape(MICRO, device_count, MB_TOK, TOP)
    mixed = jnp.einsum("msbk,msbkd->msbd", weights, picked.astype(jnp.float32))
    return mixed.reshape(MICRO, TOKENS, D).astype(jnp.bfloat16)
```

```python
import functools

import jax
import jax.numpy as jnp
from jax import lax
from jax.experimental import pallas as pl
from jax.experimental.pallas import tpu as pltpu
from jax.sharding import PartitionSpec as P

MESH = pl.DeviceIdType.MESH
LANES = 128
TILE = 256


def kernel(ring, planar, tokens, half, payload, scales, ids, codes, wg_hbm, wu_hbm, wd_hbm, out, xa, xb, hid, y0, y1, s0, s1,
           i0, i1, r0, r1, wg, wu, wd, wsem, gsend, grecv, hsend, hrecv, rsend, rrecv, psend, precv):
    T, H = tokens, ring // 2
    width = 2 * half
    row, col = lax.axis_index("row"), lax.axis_index("col")
    expert = row * ring + col
    x, y, sib, inc, got = (xa, xb), (y0, y1), (s0, s1), (i0, i1), (r0, r1)

    def column(p):
        p = (p + ring) % ring
        if planar == 1:
            return p
        back = p // H
        return 2 * (p * (1 - back) + (ring - 1 - p) * back) + back

    if planar == 1:
        place = col
    else:
        place = (col // 2) * (1 - col % 2) + (ring - 1 - col // 2) * (col % 2)
    after, before = {"col": column(place + 1)}, {"col": column(place - 1)}
    other = {"row": 1 - row}
    onward = (after, before)
    homeward = (before, after)

    weights = [
        pltpu.make_async_copy(wg_hbm.at[0], wg, wsem.at[0]),
        pltpu.make_async_copy(wu_hbm.at[0], wu, wsem.at[1]),
        pltpu.make_async_copy(wd_hbm.at[0], wd, wsem.at[2]),
    ]
    for copy in weights:
        copy.start()

    barrier = pltpu.get_barrier_semaphore()
    for device in (after, before, other):
        pl.semaphore_signal(barrier, inc=1, device_id=device, device_id_type=MESH)

    lane = lax.broadcasted_iota(jnp.int32, (T, LANES), 1)
    dense = jnp.zeros((T, LANES), jnp.float32)
    for k in range(ids.shape[1]):
        dense += jnp.where(ids[:, k : k + 1] == lane, codes[:, k : k + 1], 0).astype(jnp.float32)
    xa[0, :T, half:] = dense.astype(jnp.bfloat16)
    for j in range(width // LANES):
        value = payload[:, j * LANES : (j + 1) * LANES].astype(jnp.float32) * scales[:, j : j + 1].astype(jnp.float32)
        side, at = divmod(j * LANES, half)
        x[side][0, :T, at : at + LANES] = value.astype(jnp.bfloat16)

    def single(d):
        return d == 0 or d == H

    def rows_in(d, way):
        return pl.ds(0 if single(d) else way * T, T)

    def rows_other(d, way):
        return pl.ds(T if single(d) else 2 * T + way * T, T)

    def gather_copy(d, way, sub):
        ch = way if sub == 0 else 1 - way
        return pltpu.make_async_remote_copy(
            x[ch].at[d - 1, rows_in(d - 1, way)], x[ch].at[d, rows_in(d, way)],
            gsend.at[d, way, sub], grecv.at[d, way, sub], device_id=onward[way], device_id_type=MESH)

    def share_copy(d, way, ch):
        return pltpu.make_async_remote_copy(
            x[ch].at[d, rows_in(d, way)], x[ch].at[d, rows_other(d, way)],
            hsend.at[d, way, ch], hrecv.at[d, way, ch], device_id=other, device_id_type=MESH)

    def reduce_copy(d, way, ch):
        return pltpu.make_async_remote_copy(
            y[ch].at[d, rows_in(d, way)], got[ch].at[d - 1, pl.ds(way * T, T)],
            rsend.at[d, way, ch], rrecv.at[d, way, ch], device_id=homeward[way], device_id_type=MESH)

    def pair_copy(d, ch):
        n = T if single(d) else 2 * T
        return pltpu.make_async_remote_copy(
            sib[ch].at[d, :n], inc[ch].at[d, :n],
            psend.at[d, ch], precv.at[d, ch], device_id=other, device_id_type=MESH)

    sends = []

    def start(copy):
        copy.start()
        sends.append(copy)

    def shares(d):
        if d == 0:
            return [(0, 0), (0, 1)]
        if d == H:
            return [(0, 0), (1, 1)]
        return [(way, ch) for way in (0, 1) for ch in (0, 1)]

    def arrive(d, sub):
        for way in (0, 1):
            gather_copy(d, way, sub).wait_recv()
            if d + 1 < H or (d + 1 == H and sub == 0):
                start(gather_copy(d + 1, way, sub))
            start(share_copy(d, way, way if sub == 0 else 1 - way))

    def gate_up(d):
        for way, ch in shares(d):
            share_copy(d, way, ch).wait_recv()
        m = 2 * T if single(d) else 4 * T
        lanes = lax.broadcasted_iota(jnp.int32, (m, LANES), 1)
        picked = jnp.where(lanes == expert, xa[d, :m, half:].astype(jnp.float32), 0.0)
        code = jnp.sum(picked, axis=1, keepdims=True)

        def step(i, carry):
            c = pl.ds(pl.multiple_of(i * TILE, TILE), TILE)
            left, right = xa[d, :m, :half], xb[d, :m, :]
            g = jnp.dot(left, wg[:half, c], preferred_element_type=jnp.float32)
            g += jnp.dot(right, wg[half:, c], preferred_element_type=jnp.float32)
            u = jnp.dot(left, wu[:half, c], preferred_element_type=jnp.float32)
            u += jnp.dot(right, wu[half:, c], preferred_element_type=jnp.float32)
            hid[:m, c] = (g / (1.0 + jnp.exp(-g)) * u * code).astype(jnp.bfloat16)
            return carry

        lax.fori_loop(0, wg.shape[1] // TILE, step, 0)

    def down(d, ch):
        m = 2 * T if single(d) else 4 * T
        n = m // 2

        def step(i, carry):
            c = pl.ds(pl.multiple_of(i * TILE, TILE), TILE)
            w = pl.ds(pl.multiple_of(ch * half + i * TILE, TILE), TILE)
            o = jnp.dot(hid[:m], wd[:, w], preferred_element_type=jnp.float32).astype(jnp.bfloat16)
            y[ch][d, :n, c] = o[:n]
            sib[ch][d, :n, c] = o[n:]
            return carry

        lax.fori_loop(0, half // TILE, step, 0)
        start(pair_copy(d, ch))

    def downs(d):
        down(d, 0)
        down(d, 1)

    paired = set()

    def item(d, sub):
        for way in (0, 1):
            ch = way if sub == 0 else 1 - way
            if (d, ch) not in paired:
                pair_copy(d, ch).wait_recv()
                paired.add((d, ch))
            at = rows_in(d, way)
            total = y[ch][d, at, :].astype(jnp.float32) + inc[ch][d, at, :].astype(jnp.float32)
            if d + 1 < H or (d + 1 == H and sub == 0):
                reduce_copy(d + 1, way, ch).wait_recv()
                total += got[ch][d, pl.ds(way * T, T), :].astype(jnp.float32)
            y[ch][d, at, :] = total.astype(jnp.bfloat16)
            start(reduce_copy(d, way, ch))

    pl.semaphore_wait(barrier, 3)
    for way in (0, 1):
        start(gather_copy(1, way, 0))
    for ch in (0, 1):
        start(share_copy(0, 0, ch))
    for way in (0, 1):
        start(gather_copy(1, way, 1))

    arrive(1, 0)
    arrive(1, 1)
    weights[0].wait()
    weights[1].wait()
    gate_up(0)
    arrive(2, 0)
    weights[2].wait()
    downs(0)
    gate_up(1)
    if H > 2:
        arrive(2, 1)
    downs(1)
    for d in range(2, H):
        if d + 1 < H:
            arrive(d + 1, 0)
            gate_up(d)
            arrive(d + 1, 1)
            downs(d)
        else:
            gate_up(d)
            arrive(H, 0)
            downs(d)
    item(H - 1, 1)
    gate_up(H)
    downs(H)
    for d in range(H, 1, -1):
        item(d, 0)
        if d - 2 >= 1:
            item(d - 2, 1)
    item(1, 0)

    total_code = jnp.sum(codes[...].astype(jnp.float32), axis=1, keepdims=True)
    for ch in (0, 1):
        pair_copy(0, ch).wait_recv()
    for ch in (0, 1):
        total = y[ch][0, :T, :].astype(jnp.float32) + inc[ch][0, :T, :].astype(jnp.float32)
        for way in (1 - ch, ch):
            reduce_copy(1, way, ch).wait_recv()
            total += got[ch][0, pl.ds(way * T, T), :].astype(jnp.float32)
        out[:, ch * half : (ch + 1) * half] = (total / total_code).astype(jnp.bfloat16)
    for copy in sends:
        copy.wait_send()


def shards(ring, planar, payload, block_scales, expert_ids, gate_codes, w_gate, w_up, w_down):
    micro, local, width = payload.shape
    tokens, half, H = micro * local, width // 2, ring // 2
    hidden = w_gate.shape[2]
    flat = [a.reshape(tokens, a.shape[2]) for a in (payload, block_scales, expert_ids, gate_codes)]
    vmem, hbm = pl.BlockSpec(memory_space=pltpu.VMEM), pl.BlockSpec(memory_space=pl.ANY)
    bf16, dma = jnp.bfloat16, pltpu.SemaphoreType.DMA
    mixed = pl.pallas_call(
        functools.partial(kernel, ring, planar, tokens, half),
        out_shape=jax.ShapeDtypeStruct((tokens, width), bf16),
        in_specs=[vmem] * 4 + [hbm] * 3,
        out_specs=vmem,
        scratch_shapes=[
            pltpu.VMEM((H + 1, 4 * tokens, half + LANES), bf16),
            pltpu.VMEM((H + 1, 4 * tokens, half), bf16),
            pltpu.VMEM((4 * tokens, hidden), bf16),
            *[pltpu.VMEM((H + 1, 2 * tokens, half), bf16)] * 6,
            *[pltpu.VMEM((H, 2 * tokens, half), bf16)] * 2,
            pltpu.VMEM((width, hidden), bf16),
            pltpu.VMEM((width, hidden), bf16),
            pltpu.VMEM((hidden, width), bf16),
            dma((3,)),
            *[dma((H + 1, 2, 2))] * 6,
            *[dma((H + 1, 2))] * 2,
        ],
        compiler_params=pltpu.CompilerParams(
            collective_id=0, has_side_effects=True, vmem_limit_bytes=62 * 1024 * 1024
        ),
    )(*flat, w_gate, w_up, w_down)
    return mixed.reshape(micro, local, width)


def solution(mesh):
    ring = mesh.shape["col"]
    planar = max(1, 4 // mesh.shape["groups"])
    spread = P(None, ("groups", "row", "col"), None)
    placed = P(("row", "col"), None, None)
    return jax.shard_map(
        functools.partial(shards, ring, planar),
        mesh=mesh,
        in_specs=(spread,) * 4 + (placed,) * 3,
        out_specs=spread,
        check_vma=False,
    )
```

```python
import functools

import jax
import jax.numpy as jnp
from jax import lax
from jax.experimental import pallas as pl
from jax.experimental.pallas import tpu as pltpu
from jax.sharding import PartitionSpec as P

MESH = pl.DeviceIdType.MESH
LANES = 128
TILE = 512


def kernel(ring, planar, tokens, half, payload, scales, ids, codes, wg_hbm, wu_hbm, wd_hbm, out, xa, xb, hid, y0, y1, s0, s1,
           i0, i1, r0, r1, wg, wu, wd, wsem, gsend, grecv, hsend, hrecv, rsend, rrecv, psend, precv):
    T, H = tokens, ring // 2
    width = 2 * half
    row, col = lax.axis_index("row"), lax.axis_index("col")
    expert = row * ring + col
    x, y, sib, inc, got = (xa, xb), (y0, y1), (s0, s1), (i0, i1), (r0, r1)

    def column(p):
        p = (p + ring) % ring
        if planar == 1:
            return p
        back = p // H
        return 2 * (p * (1 - back) + (ring - 1 - p) * back) + back

    if planar == 1:
        place = col
    else:
        place = (col // 2) * (1 - col % 2) + (ring - 1 - col // 2) * (col % 2)
    after, before = {"col": column(place + 1)}, {"col": column(place - 1)}
    other = {"row": 1 - row}
    onward = (after, before)
    homeward = (before, after)

    weights = [
        pltpu.make_async_copy(wg_hbm.at[0], wg, wsem.at[0]),
        pltpu.make_async_copy(wu_hbm.at[0], wu, wsem.at[1]),
        pltpu.make_async_copy(wd_hbm.at[0], wd, wsem.at[2]),
    ]
    for copy in weights:
        copy.start()

    barrier = pltpu.get_barrier_semaphore()
    for device in (after, before, other):
        pl.semaphore_signal(barrier, inc=1, device_id=device, device_id_type=MESH)

    local = T // ids.shape[0]
    lane = lax.broadcasted_iota(jnp.int32, (local, LANES), 1)
    parts, sums = [], []
    for micro in range(ids.shape[0]):
        named, code = jnp.swapaxes(ids[micro], 0, 1), jnp.swapaxes(codes[micro], 0, 1)
        dense = jnp.zeros((local, LANES), jnp.float32)
        for k in range(named.shape[1]):
            dense += jnp.where(named[:, k : k + 1] == lane, code[:, k : k + 1], 0).astype(jnp.float32)
        parts.append(dense)
    dense = jnp.concatenate(parts, axis=0)
    inverse = 1.0 / jnp.sum(dense, axis=1, keepdims=True)
    xa[0, :T, half:] = dense.astype(jnp.bfloat16)

    def dequantize(side):
        for j in range(half // LANES):
            at, block = side * half + j * LANES, side * (half // LANES) + j
            value = payload[:, at : at + LANES].astype(jnp.float32) * scales[:, block : block + 1].astype(jnp.float32)
            x[side][0, :T, j * LANES : (j + 1) * LANES] = value.astype(jnp.bfloat16)

    def single(d):
        return d == 0 or d == H

    def rows_in(d, way):
        return pl.ds(0 if single(d) else way * T, T)

    def rows_other(d, way):
        return pl.ds(T if single(d) else 2 * T + way * T, T)

    def gather_copy(d, way, sub):
        ch = way if sub == 0 else 1 - way
        return pltpu.make_async_remote_copy(
            x[ch].at[d - 1, rows_in(d - 1, way)], x[ch].at[d, rows_in(d, way)],
            gsend.at[d, way, sub], grecv.at[d, way, sub], device_id=onward[way], device_id_type=MESH)

    def share_copy(d, way, ch):
        return pltpu.make_async_remote_copy(
            x[ch].at[d, rows_in(d, way)], x[ch].at[d, rows_other(d, way)],
            hsend.at[d, way, ch], hrecv.at[d, way, ch], device_id=other, device_id_type=MESH)

    def reduce_copy(d, way, ch):
        return pltpu.make_async_remote_copy(
            y[ch].at[d, rows_in(d, way)], got[ch].at[d - 1, pl.ds(way * T, T)],
            rsend.at[d, way, ch], rrecv.at[d, way, ch], device_id=homeward[way], device_id_type=MESH)

    def pair_copy(d, ch):
        n = T if single(d) else 2 * T
        return pltpu.make_async_remote_copy(
            sib[ch].at[d, :n], inc[ch].at[d, :n],
            psend.at[d, ch], precv.at[d, ch], device_id=other, device_id_type=MESH)

    sends = []

    def start(copy):
        copy.start()
        sends.append(copy)

    def shares(d):
        if d == 0:
            return [(0, 0), (0, 1)]
        if d == H:
            return [(0, 0), (1, 1)]
        return [(way, ch) for way in (0, 1) for ch in (0, 1)]

    def arrive(d, sub):
        for way in (0, 1):
            gather_copy(d, way, sub).wait_recv()
            if d + 1 < H or (d + 1 == H and sub == 0):
                start(gather_copy(d + 1, way, sub))
            start(share_copy(d, way, way if sub == 0 else 1 - way))

    def gate_up(d):
        for way, ch in shares(d):
            share_copy(d, way, ch).wait_recv()
        m = 2 * T if single(d) else 4 * T
        lanes = lax.broadcasted_iota(jnp.int32, (m, LANES), 1)
        picked = jnp.where(lanes == expert, xa[d, :m, half:].astype(jnp.float32), 0.0)
        code = jnp.sum(picked, axis=1, keepdims=True)

        def step(i, carry):
            c = pl.ds(pl.multiple_of(i * TILE, TILE), TILE)
            left, right = xa[d, :m, :half], xb[d, :m, :]
            g = jnp.dot(left, wg[:half, c], preferred_element_type=jnp.float32)
            g += jnp.dot(right, wg[half:, c], preferred_element_type=jnp.float32)
            u = jnp.dot(left, wu[:half, c], preferred_element_type=jnp.float32)
            u += jnp.dot(right, wu[half:, c], preferred_element_type=jnp.float32)
            hid[:m, c] = (g / (1.0 + jnp.exp(-g)) * u * code).astype(jnp.bfloat16)
            return carry

        lax.fori_loop(0, wg.shape[1] // TILE, step, 0)

    def down(d, ch):
        m = 2 * T if single(d) else 4 * T
        n = m // 2

        w = wd[:, ch * half : (ch + 1) * half]
        o = jnp.dot(hid[:m], w, preferred_element_type=jnp.float32).astype(jnp.bfloat16)
        y[ch][d, :n, :] = o[:n]
        sib[ch][d, :n, :] = o[n:]
        start(pair_copy(d, ch))

    def downs(d):
        down(d, 0)
        down(d, 1)

    paired = set()

    def item(d, sub):
        for way in (0, 1):
            ch = way if sub == 0 else 1 - way
            if (d, ch) not in paired:
                pair_copy(d, ch).wait_recv()
                paired.add((d, ch))
            at = rows_in(d, way)
            total = y[ch][d, at, :].astype(jnp.float32) + inc[ch][d, at, :].astype(jnp.float32)
            if d + 1 < H or (d + 1 == H and sub == 0):
                reduce_copy(d + 1, way, ch).wait_recv()
                total += got[ch][d, pl.ds(way * T, T), :].astype(jnp.float32)
            y[ch][d, at, :] = total.astype(jnp.bfloat16)
            start(reduce_copy(d, way, ch))

    for way in (0, 1):
        dequantize(way)
        if way == 0:
            pl.semaphore_wait(barrier, 3)
        start(gather_copy(1, way, 0))
    for ch in (0, 1):
        start(share_copy(0, 0, ch))
    for way in (0, 1):
        start(gather_copy(1, way, 1))

    arrive(1, 0)
    arrive(1, 1)
    weights[0].wait()
    weights[1].wait()
    gate_up(0)
    arrive(2, 0)
    weights[2].wait()
    downs(0)
    gate_up(1)
    if H > 2:
        arrive(2, 1)
    downs(1)
    for d in range(2, H):
        if d + 1 < H:
            arrive(d + 1, 0)
            gate_up(d)
            arrive(d + 1, 1)
            downs(d)
        else:
            gate_up(d)
            arrive(H, 0)
            downs(d)
    item(H - 1, 1)
    gate_up(H)
    downs(H)
    for d in range(H, 1, -1):
        item(d, 0)
        if d - 2 >= 1:
            item(d - 2, 1)
    item(1, 0)

    for ch in (0, 1):
        pair_copy(0, ch).wait_recv()
    for ch in (0, 1):
        total = y[ch][0, :T, :].astype(jnp.float32) + inc[ch][0, :T, :].astype(jnp.float32)
        for way in (1 - ch, ch):
            reduce_copy(1, way, ch).wait_recv()
            total += got[ch][0, pl.ds(way * T, T), :].astype(jnp.float32)
        out[:, ch * half : (ch + 1) * half] = (total * inverse).astype(jnp.bfloat16)
    for copy in sends:
        copy.wait_send()


def shards(ring, planar, payload, block_scales, expert_ids, gate_codes, w_gate, w_up, w_down):
    micro, local, width = payload.shape
    tokens, half, H = micro * local, width // 2, ring // 2
    hidden = w_gate.shape[2]
    flat = [a.reshape(tokens, a.shape[2]) for a in (payload, block_scales)]
    flat += [jnp.swapaxes(a, 1, 2) for a in (expert_ids, gate_codes)]
    vmem, hbm = pl.BlockSpec(memory_space=pltpu.VMEM), pl.BlockSpec(memory_space=pl.ANY)
    bf16, dma = jnp.bfloat16, pltpu.SemaphoreType.DMA
    mixed = pl.pallas_call(
        functools.partial(kernel, ring, planar, tokens, half),
        out_shape=jax.ShapeDtypeStruct((tokens, width), bf16),
        in_specs=[vmem] * 4 + [hbm] * 3,
        out_specs=vmem,
        scratch_shapes=[
            pltpu.VMEM((H + 1, 4 * tokens, half + LANES), bf16),
            pltpu.VMEM((H + 1, 4 * tokens, half), bf16),
            pltpu.VMEM((4 * tokens, hidden), bf16),
            *[pltpu.VMEM((H + 1, 2 * tokens, half), bf16)] * 6,
            *[pltpu.VMEM((H, 2 * tokens, half), bf16)] * 2,
            pltpu.VMEM((width, hidden), bf16),
            pltpu.VMEM((width, hidden), bf16),
            pltpu.VMEM((hidden, width), bf16),
            dma((3,)),
            *[dma((H + 1, 2, 2))] * 6,
            *[dma((H + 1, 2))] * 2,
        ],
        compiler_params=pltpu.CompilerParams(
            collective_id=0, has_side_effects=True, vmem_limit_bytes=62 * 1024 * 1024
        ),
    )(*flat, w_gate, w_up, w_down)
    return mixed.reshape(micro, local, width)


def solution(mesh):
    ring = mesh.shape["col"]
    planar = max(1, 4 // mesh.shape["groups"])
    spread = P(None, ("groups", "row", "col"), None)
    placed = P(("row", "col"), None, None)
    return jax.shard_map(
        functools.partial(shards, ring, planar),
        mesh=mesh,
        in_specs=(spread,) * 4 + (placed,) * 3,
        out_specs=spread,
        check_vma=False,
    )
```

```python
import functools

import jax
import jax.numpy as jnp
from jax import lax
from jax.experimental import pallas as pl
from jax.experimental.pallas import tpu as pltpu
from jax.sharding import PartitionSpec as P

MESH = pl.DeviceIdType.MESH
LANES = 128
TILE = 512


def kernel(ring, planar, tokens, half, payload, scales, ids, codes, wg_hbm, wu_hbm, wd_hbm, out, xa, xb, hid, y0, y1, s0, s1,
           i0, i1, r0, r1, wg, wu, wd, wsem, gsend, grecv, hsend, hrecv, rsend, rrecv, psend, precv):
    T, H = tokens, ring // 2
    width = 2 * half
    row, col = lax.axis_index("row"), lax.axis_index("col")
    expert = row * ring + col
    x, y, sib, inc, got = (xa, xb), (y0, y1), (s0, s1), (i0, i1), (r0, r1)

    def column(p):
        p = (p + ring) % ring
        if planar == 1:
            return p
        back = p // H
        return 2 * (p * (1 - back) + (ring - 1 - p) * back) + back

    if planar == 1:
        place = col
    else:
        place = (col // 2) * (1 - col % 2) + (ring - 1 - col // 2) * (col % 2)
    after, before = {"col": column(place + 1)}, {"col": column(place - 1)}
    other = {"row": 1 - row}
    onward = (after, before)
    homeward = (before, after)

    weights = [
        pltpu.make_async_copy(wg_hbm.at[0], wg, wsem.at[0]),
        pltpu.make_async_copy(wu_hbm.at[0], wu, wsem.at[1]),
        pltpu.make_async_copy(wd_hbm.at[0], wd, wsem.at[2]),
    ]
    for copy in weights:
        copy.start()

    barrier = pltpu.get_barrier_semaphore()
    for device in (after, before, other):
        pl.semaphore_signal(barrier, inc=1, device_id=device, device_id_type=MESH)

    local = T // ids.shape[0]
    lane = lax.broadcasted_iota(jnp.int32, (local, LANES), 1)
    parts, sums = [], []
    for micro in range(ids.shape[0]):
        named, code = jnp.swapaxes(ids[micro], 0, 1), jnp.swapaxes(codes[micro], 0, 1)
        dense = jnp.zeros((local, LANES), jnp.float32)
        for k in range(named.shape[1]):
            dense += jnp.where(named[:, k : k + 1] == lane, code[:, k : k + 1], 0).astype(jnp.float32)
        parts.append(dense)
    dense = jnp.concatenate(parts, axis=0)
    inverse = 1.0 / jnp.sum(dense, axis=1, keepdims=True)
    xa[0, :T, half:] = dense.astype(jnp.bfloat16)

    def dequantize(side):
        for j in range(half // LANES):
            at, block = side * half + j * LANES, side * (half // LANES) + j
            value = payload[:, at : at + LANES].astype(jnp.float32) * scales[:, block : block + 1].astype(jnp.float32)
            x[side][0, :T, j * LANES : (j + 1) * LANES] = value.astype(jnp.bfloat16)

    def single(d):
        return d == 0 or d == H

    def rows_in(d, way):
        return pl.ds(0 if single(d) else way * T, T)

    def rows_other(d, way):
        return pl.ds(T if single(d) else 2 * T + way * T, T)

    def gather_copy(d, way, sub):
        ch = way if sub == 0 else 1 - way
        return pltpu.make_async_remote_copy(
            x[ch].at[d - 1, rows_in(d - 1, way)], x[ch].at[d, rows_in(d, way)],
            gsend.at[d, way, sub], grecv.at[d, way, sub], device_id=onward[way], device_id_type=MESH)

    def share_copy(d, way, ch):
        return pltpu.make_async_remote_copy(
            x[ch].at[d, rows_in(d, way)], x[ch].at[d, rows_other(d, way)],
            hsend.at[d, way, ch], hrecv.at[d, way, ch], device_id=other, device_id_type=MESH)

    def reduce_copy(d, way, ch):
        return pltpu.make_async_remote_copy(
            y[ch].at[d, rows_in(d, way)], got[ch].at[d - 1, pl.ds(way * T, T)],
            rsend.at[d, way, ch], rrecv.at[d, way, ch], device_id=homeward[way], device_id_type=MESH)

    def pair_copy(d, ch):
        n = T if single(d) else 2 * T
        return pltpu.make_async_remote_copy(
            sib[ch].at[d, :n], inc[ch].at[d, :n],
            psend.at[d, ch], precv.at[d, ch], device_id=other, device_id_type=MESH)

    sends = []

    def start(copy):
        copy.start()
        sends.append(copy)

    def shares(d):
        if d == 0:
            return [(0, 0), (0, 1)]
        if d == H:
            return [(0, 0), (1, 1)]
        return [(way, ch) for way in (0, 1) for ch in (0, 1)]

    def arrive(d, sub):
        for way in (0, 1):
            gather_copy(d, way, sub).wait_recv()
            if d + 1 < H or (d + 1 == H and sub == 0):
                start(gather_copy(d + 1, way, sub))
            start(share_copy(d, way, way if sub == 0 else 1 - way))

    def gate_up(d):
        for way, ch in shares(d):
            share_copy(d, way, ch).wait_recv()
        m = 2 * T if single(d) else 4 * T
        lanes = lax.broadcasted_iota(jnp.int32, (m, LANES), 1)
        picked = jnp.where(lanes == expert, xa[d, :m, half:].astype(jnp.float32), 0.0)
        code = jnp.sum(picked, axis=1, keepdims=True)

        def step(i, carry):
            c = pl.ds(pl.multiple_of(i * TILE, TILE), TILE)
            left, right = xa[d, :m, :half], xb[d, :m, :]
            g = jnp.dot(left, wg[:half, c], preferred_element_type=jnp.float32)
            g += jnp.dot(right, wg[half:, c], preferred_element_type=jnp.float32)
            u = jnp.dot(left, wu[:half, c], preferred_element_type=jnp.float32)
            u += jnp.dot(right, wu[half:, c], preferred_element_type=jnp.float32)
            hid[d % 3, :m, c] = (g / (1.0 + jnp.exp(-g)) * u * code).astype(jnp.bfloat16)
            return carry

        lax.fori_loop(0, wg.shape[1] // TILE, step, 0)

    def down(d, ch):
        m = 2 * T if single(d) else 4 * T
        n = m // 2

        w = wd[:, ch * half : (ch + 1) * half]
        o = jnp.dot(hid[d % 3, :m], w, preferred_element_type=jnp.float32).astype(jnp.bfloat16)
        y[ch][d, :n, :] = o[:n]
        sib[ch][d, :n, :] = o[n:]
        start(pair_copy(d, ch))

    def downs(d):
        down(d, 0)
        down(d, 1)

    paired = set()

    def item(d, sub):
        for way in (0, 1):
            ch = way if sub == 0 else 1 - way
            if (d, ch) not in paired:
                pair_copy(d, ch).wait_recv()
                paired.add((d, ch))
            at = rows_in(d, way)
            total = y[ch][d, at, :].astype(jnp.float32) + inc[ch][d, at, :].astype(jnp.float32)
            if d + 1 < H or (d + 1 == H and sub == 0):
                reduce_copy(d + 1, way, ch).wait_recv()
                total += got[ch][d, pl.ds(way * T, T), :].astype(jnp.float32)
            y[ch][d, at, :] = total.astype(jnp.bfloat16)
            start(reduce_copy(d, way, ch))

    for way in (0, 1):
        dequantize(way)
        if way == 0:
            pl.semaphore_wait(barrier, 3)
        start(gather_copy(1, way, 0))
    for ch in (0, 1):
        start(share_copy(0, 0, ch))
    for way in (0, 1):
        start(gather_copy(1, way, 1))

    arrive(1, 0)
    arrive(1, 1)
    weights[0].wait()
    weights[1].wait()
    gate_up(0)
    arrive(2, 0)
    weights[2].wait()
    downs(0)
    gate_up(1)
    if H > 2:
        arrive(2, 1)
    downs(1)
    for d in range(2, H):
        if d + 1 < H:
            arrive(d + 1, 0)
            gate_up(d)
            arrive(d + 1, 1)
            if d < H - 2:
                downs(d)
        else:
            gate_up(d)
            arrive(H, 0)
            downs(d)
    item(H - 1, 1)
    gate_up(H)
    downs(H)
    for d in range(H, 1, -1):
        item(d, 0)
        if d == H and H >= 4:
            downs(H - 2)
        if d - 2 >= 1:
            item(d - 2, 1)
    item(1, 0)

    for ch in (0, 1):
        pair_copy(0, ch).wait_recv()
    for ch in (0, 1):
        total = y[ch][0, :T, :].astype(jnp.float32) + inc[ch][0, :T, :].astype(jnp.float32)
        for way in (1 - ch, ch):
            reduce_copy(1, way, ch).wait_recv()
            total += got[ch][0, pl.ds(way * T, T), :].astype(jnp.float32)
        out[:, ch * half : (ch + 1) * half] = (total * inverse).astype(jnp.bfloat16)
    for copy in sends:
        copy.wait_send()


def shards(ring, planar, payload, block_scales, expert_ids, gate_codes, w_gate, w_up, w_down):
    micro, local, width = payload.shape
    tokens, half, H = micro * local, width // 2, ring // 2
    hidden = w_gate.shape[2]
    flat = [a.reshape(tokens, a.shape[2]) for a in (payload, block_scales)]
    flat += [jnp.swapaxes(a, 1, 2) for a in (expert_ids, gate_codes)]
    vmem, hbm = pl.BlockSpec(memory_space=pltpu.VMEM), pl.BlockSpec(memory_space=pl.ANY)
    bf16, dma = jnp.bfloat16, pltpu.SemaphoreType.DMA
    mixed = pl.pallas_call(
        functools.partial(kernel, ring, planar, tokens, half),
        out_shape=jax.ShapeDtypeStruct((tokens, width), bf16),
        in_specs=[vmem] * 4 + [hbm] * 3,
        out_specs=vmem,
        scratch_shapes=[
            pltpu.VMEM((H + 1, 4 * tokens, half + LANES), bf16),
            pltpu.VMEM((H + 1, 4 * tokens, half), bf16),
            pltpu.VMEM((3, 4 * tokens, hidden), bf16),
            *[pltpu.VMEM((H + 1, 2 * tokens, half), bf16)] * 6,
            *[pltpu.VMEM((H, 2 * tokens, half), bf16)] * 2,
            pltpu.VMEM((width, hidden), bf16),
            pltpu.VMEM((width, hidden), bf16),
            pltpu.VMEM((hidden, width), bf16),
            dma((3,)),
            *[dma((H + 1, 2, 2))] * 6,
            *[dma((H + 1, 2))] * 2,
        ],
        compiler_params=pltpu.CompilerParams(
            collective_id=0, has_side_effects=True, vmem_limit_bytes=62 * 1024 * 1024
        ),
    )(*flat, w_gate, w_up, w_down)
    return mixed.reshape(micro, local, width)


def solution(mesh):
    ring = mesh.shape["col"]
    planar = max(1, 4 // mesh.shape["groups"])
    spread = P(None, ("groups", "row", "col"), None)
    placed = P(("row", "col"), None, None)
    return jax.shard_map(
        functools.partial(shards, ring, planar),
        mesh=mesh,
        in_specs=(spread,) * 4 + (placed,) * 3,
        out_specs=spread,
        check_vma=False,
    )
```
